32 devices in a mesh: kv: 2 (over core), page: 16 (over z, y, x).
Axes of the slice: x: 2, y: 2, z: 4, core: 2. Of those that a mesh axis runs over, the one named last changes fastest.
Arguments:
- tokens: bfloat16 [4096, 2048], P('page'), may hold values from -6 to 6
- in_gain: float32 [2048], replicated, may hold values from 0.4 to 1.6
- w_query: bfloat16 [2048, 2048], P(None, 'kv'), may hold values from -0.125 to 0.125
- key_projection_weight: bfloat16 [2048, 512], P(None, 'kv'), may hold values from -0.125 to 0.125
- value_projection_weight: bfloat16 [2048, 512], P(None, 'kv'), may hold values from -0.125 to 0.125
- q_gain: float32 [256], replicated, may hold values from 0.5 to 6
- k_gain: float32 [256], replicated, may hold values from 0.4 to 1.6
- w_out: bfloat16 [2048, 2048], P('kv'), may hold values from -0.125 to 0.125
- post_gain: float32 [2048], replicated, may hold values from 0.25 to 1.75
- laurel_left: bfloat16 [2048, 64], replicated, may hold values from -0.125 to 0.125
- laurel_right: bfloat16 [64, 2048], replicated, may hold values from -0.75 to 0.75
- laurel_gain: float32 [2048], replicated, may hold values from 0.25 to 1.75
- prefix_key_slots: bfloat16 [16384, 512], P('page', 'kv'), may hold values from -20 to 20
- prefix_value_slots: bfloat16 [16384, 512], P('page', 'kv'), may hold values from -6 to 6
- prefix_slot_map: int32 [128], replicated, may hold values from 0 to 127, each once
- page_lengths: int32 [8], replicated, may hold values from 1 to 8, 32 in all
- request_group: int32 [8], replicated, may hold values from 0 to 3
- suffix_page_map: int32 [32], P('page'), may hold values from 0 to 31, as said below
Outputs:
- layer_out: bfloat16 [4096, 2048], P('page', 'kv')
- suffix_key_cache: bfloat16 [4096, 512], P('page', 'kv')
- suffix_value_cache: bfloat16 [4096, 512], P('page', 'kv')
The draws below stay inside these ranges and needn't reach their ends.
Inputs may be any that keep to these rules, and one draw needn't show every extreme that they name: `prefix_slot_map`: A permutation: entry g * 32 + j names the page slot (rows of 128 tokens of prefix_key_slots and prefix_value_slots) that holds page j of prefix g. `page_lengths`: they sum to 32; some request has exactly 8 pages. `suffix_page_map`: A permutation that keeps every logical page within the aligned block of 2 pages that contains it.
All inputs are finite; a program needn't handle non-finite values.
Results may differ from the reference program's by a relative error of at most 0.01.
The reference program's roundings to bfloat16 on the way count: a program that leaves them out, or rounds other values in their place, can miss the bound.
Values may be sent and summed in bfloat16 or wider, within the bound.
A program may use at most 128 MiB of HBM per device.

```python
import math
import jax
import jax.numpy as jnp
import numpy as np
from jax import lax

MODEL_DIM = 2048
QUERY_HEADS = 8
KEY_VALUE_HEADS = 2
HEAD_SIZE = 256
RANK = 64
PAGE_TOKENS = 128
PREFIX_TOKENS = 4096
PREFIX_COUNT = 4
MAXP = 8
PAGES_DEV = 2
PREFIX_PAGES = 32
SUFFIX_PAGES = 32
SUFFIX_TOKENS = 4096
REQS = 8


def draw_q_gain(key, part):
    return jax.random.uniform(key, (HEAD_SIZE,), jnp.float32, 0.5, 1.5)


def draw_prefix_key_slots(key, part):
    start_offset = jax.random.normal(jax.random.fold_in(key, 11), (PREFIX_COUNT * PREFIX_TOKENS, KEY_VALUE_HEADS * HEAD_SIZE), jnp.float32)
    start_offset = jnp.clip(start_offset, -6.0, 6.0)
    column_scale_factor = jax.random.uniform(jax.random.fold_in(key, 13), (1, KEY_VALUE_HEADS * HEAD_SIZE), jnp.float32, 0.4, 1.6)
    start_offset = start_offset * column_scale_factor
    return start_offset.astype(jnp.bfloat16)


def draw_suffix_page_map(key, part):
    blocks = SUFFIX_PAGES // PAGES_DEV
    block_keys = jax.random.split(jax.random.fold_in(key, 21), blocks)
    orders = jax.vmap(lambda block_key: jax.random.permutation(block_key, PAGES_DEV))(block_keys)
    return (orders + (jnp.arange(blocks) * PAGES_DEV)[:, None]).reshape(SUFFIX_PAGES).astype(jnp.int32)


def plant(drawn, key, smallest, high):
    index_at = [jax.random.randint(jax.random.fold_in(key, axis), (), 0, length) for axis, length in enumerate(drawn.shape)]
    widest = drawn.shape.index(max(drawn.shape))
    neighbour = index_at[:widest] + [(index_at[widest] + 1) % drawn.shape[widest]] + index_at[widest + 1:]
    return drawn.at[tuple(index_at)].set(smallest).at[tuple(neighbour)].set(high)


def shard_levels(key, extent, shards, least, largest):
    loudness = 1.0
    for axis_at, blocks in shards:
        draws = jax.random.uniform(jax.random.fold_in(jax.random.fold_in(key, 6), axis_at), (blocks,), jnp.float32, least / len(shards), largest / len(shards))
        loudness = loudness * jnp.repeat(jnp.exp(draws), extent[axis_at] // blocks).reshape((-1,) + (1,) * (len(extent) - 1 - axis_at))
    return loudness


def split_up(count, total, limit, slope):
    portions = [(1 << 20) // math.isqrt(rank ** slope) + 1 for rank in range(2, count + 1)]
    surplus, counts = total - limit - (count - 1), [1] * (count - 1)
    while surplus > 0:
        free = [i for i in range(count - 1) if counts[i] < limit]
        whole, remaining = sum([portions[i] for i in free]), surplus
        for i in free:
            extra = min(limit - counts[i], max(1, remaining * portions[i] // whole), surplus)
            counts[i] = counts[i] + extra
            surplus = surplus - extra
    return np.array([limit] + counts)


def uneven(stream_key, count, total, bound, skew):
    if count == 2:
        one = jax.random.randint(stream_key, (), max(1, total - bound), min(bound, total - 1) + 1)
        return jnp.stack([one, total - one])
    lengths = jnp.asarray(split_up(count, total, bound, skew), jnp.int32)
    pairs = (count - 1) // 2
    source_of, sink = lengths[1:1 + 2 * pairs:2], lengths[2:2 + 2 * pairs:2]
    room = jnp.minimum(source_of - 1, bound - sink)
    shifted = jax.random.randint(jax.random.fold_in(stream_key, 1), (pairs,), 0, 1 << 20) % (room + 1)
    lengths = lengths.at[1:1 + 2 * pairs:2].set(source_of - shifted).at[2:2 + 2 * pairs:2].set(sink + shifted)
    return lengths[jax.random.permutation(jax.random.fold_in(stream_key, 2), count)]


def normal_values(own_key, extent, deviation, reach, cuts=(), kind=jnp.bfloat16):
    array = deviation * jax.random.normal(own_key, extent, jnp.float32)
    if cuts:
        array = array * shard_levels(own_key, extent, cuts, -0.22, 0.18)
    return jnp.clip(array, -reach, reach).astype(kind)


def setup_inputs(seed: int = 0) -> dict:
    key_of = jax.random.split(jax.random.key(seed), 19)
    tokens = normal_values(key_of[0], (SUFFIX_TOKENS, MODEL_DIM), 1.0, 6.0, ((0, 16),))
    in_gain = jnp.clip(1.0 + 0.12 * jax.random.normal(key_of[1], (MODEL_DIM,), jnp.float32), 0.4, 1.6)
    w_query = normal_values(key_of[2], (MODEL_DIM, QUERY_HEADS * HEAD_SIZE), MODEL_DIM ** -0.5, 0.125, ((1, 2),))
    key_projection_weight = normal_values(key_of[3], (MODEL_DIM, KEY_VALUE_HEADS * HEAD_SIZE), MODEL_DIM ** -0.5, 0.125, ((1, 2),))
    value_projection_weight = normal_values(key_of[4], (MODEL_DIM, KEY_VALUE_HEADS * HEAD_SIZE), MODEL_DIM ** -0.5, 0.125, ((1, 2),))
    q_gain = draw_q_gain(jax.random.fold_in(key_of[18], 71), 0)
    k_gain = jnp.clip(1.0 + 0.12 * jax.random.normal(key_of[6], (HEAD_SIZE,), jnp.float32), 0.4, 1.6)
    w_out = normal_values(key_of[7], (QUERY_HEADS * HEAD_SIZE, MODEL_DIM), (QUERY_HEADS * HEAD_SIZE) ** -0.5, 0.125, ((0, 2),))
    post_gain = jnp.clip(1.0 + 0.15 * jax.random.normal(key_of[8], (MODEL_DIM,), jnp.float32), 0.25, 1.75)
    laurel_left = normal_values(key_of[9], (MODEL_DIM, RANK), MODEL_DIM ** -0.5, 0.125)
    laurel_right = normal_values(key_of[10], (RANK, MODEL_DIM), RANK ** -0.5, 0.75)
    laurel_gain = jnp.clip(1.0 + 0.15 * jax.random.normal(key_of[11], (MODEL_DIM,), jnp.float32), 0.25, 1.75)
    prefix_key_slots = draw_prefix_key_slots(jax.random.fold_in(key_of[18], 71), 0)
    prefix_value_slots = normal_values(key_of[13], (PREFIX_COUNT * PREFIX_TOKENS, KEY_VALUE_HEADS * HEAD_SIZE), 1.0, 6.0, ((0, 16), (1, 2)))
    prefix_slot_map = jax.random.permutation(key_of[14], PREFIX_COUNT * PREFIX_PAGES).astype(jnp.int32)
    page_lengths = uneven(key_of[15], REQS, SUFFIX_PAGES, MAXP, 2).astype(jnp.int32)
    request_group = plant(jax.random.randint(key_of[16], (REQS,), 0, PREFIX_COUNT), jax.random.fold_in(key_of[16], 1), 0, PREFIX_COUNT - 1).astype(jnp.int32)
    suffix_page_map = draw_suffix_page_map(jax.random.fold_in(key_of[18], 71), 0)
    return {"tokens": tokens, "in_gain": in_gain, "w_query": w_query, "key_projection_weight": key_projection_weight, "value_projection_weight": value_projection_weight, "q_gain": q_gain, "k_gain": k_gain, "w_out": w_out, "post_gain": post_gain, "laurel_left": laurel_left, "laurel_right": laurel_right, "laurel_gain": laurel_gain, "prefix_key_slots": prefix_key_slots, "prefix_value_slots": prefix_value_slots, "prefix_slot_map": prefix_slot_map, "page_lengths": page_lengths, "request_group": request_group, "suffix_page_map": suffix_page_map}


epsilon = 1e-06
rope_base = 1000000.0
masked_low = -1e+30

def rms_scale(values):
    return lax.rsqrt(lax.optimization_barrier(jnp.mean(values * values, axis=-1, keepdims=True)) + epsilon)

def rotate(values, positions):
    half_dim = values.shape[-1] // 2
    inv_freq = rope_base ** (-(jnp.arange(half_dim).astype(jnp.float32) * 2.0 / values.shape[-1]))
    angles = positions.astype(jnp.float32)[:, None] * inv_freq[None, :]
    cosine = jnp.cos(angles)[:, None, :]
    sines = jnp.sin(angles)[:, None, :]
    first_half = values[..., :half_dim]
    second_half = values[..., half_dim:]
    return jnp.concatenate([first_half * cosine - second_half * sines, second_half * cosine + first_half * sines], axis=-1)

def project(tokens, in_gain, w_query, key_projection_weight, value_projection_weight, q_gain, k_gain, positions):
    tok_count = tokens.shape[0]
    tokens_wide = tokens.astype(jnp.float32)
    normed = (tokens_wide * rms_scale(tokens_wide) * in_gain).astype(jnp.bfloat16)
    queries = jnp.dot(normed, w_query, preferred_element_type=jnp.float32).reshape(tok_count, -1, HEAD_SIZE)
    queries = rotate(queries * rms_scale(queries) * q_gain, positions).astype(jnp.bfloat16)
    fresh_key_rows = jnp.dot(normed, key_projection_weight, preferred_element_type=jnp.float32).reshape(tok_count, -1, HEAD_SIZE)
    fresh_key_rows = rotate(fresh_key_rows * rms_scale(fresh_key_rows) * k_gain, positions).astype(jnp.bfloat16)
    fresh_value_rows = jnp.dot(normed, value_projection_weight, preferred_element_type=jnp.float32).reshape(tok_count, -1, HEAD_SIZE)
    fresh_value_rows = (fresh_value_rows * rms_scale(fresh_value_rows)).astype(jnp.bfloat16)
    return (normed, queries, fresh_key_rows, fresh_value_rows)

def reference(tokens, in_gain, w_query, key_projection_weight, value_projection_weight, q_gain, k_gain, w_out, post_gain, laurel_left, laurel_right, laurel_gain, prefix_key_slots, prefix_value_slots, prefix_slot_map, page_lengths, request_group, suffix_page_map):
    tok_ids = jnp.arange(SUFFIX_TOKENS, dtype=jnp.int32)
    page_starts = (jnp.cumsum(page_lengths) - page_lengths).astype(jnp.int32)
    page_of = tok_ids // PAGE_TOKENS
    belongs = ((page_of[:, None] >= page_starts[None, :]) & (page_of[:, None] < (page_starts + page_lengths)[None, :])).astype(jnp.int32)
    positions = (PREFIX_TOKENS + tok_ids - lax.optimization_barrier(jnp.sum(belongs * page_starts[None, :], axis=1)) * PAGE_TOKENS).astype(jnp.int32)
    normed, queries, fresh_key_rows, fresh_value_rows = project(tokens, in_gain, w_query, key_projection_weight, value_projection_weight, q_gain, k_gain, positions)
    sliding_window_rows = MAXP * PAGE_TOKENS
    padded_query = jnp.concatenate([queries, jnp.zeros((sliding_window_rows, QUERY_HEADS, HEAD_SIZE), jnp.bfloat16)], axis=0)
    key_with_padding = jnp.concatenate([fresh_key_rows, jnp.zeros((sliding_window_rows, KEY_VALUE_HEADS, HEAD_SIZE), jnp.bfloat16)], axis=0)
    value_with_padding = jnp.concatenate([fresh_value_rows, jnp.zeros((sliding_window_rows, KEY_VALUE_HEADS, HEAD_SIZE), jnp.bfloat16)], axis=0)
    key_by_group = prefix_key_slots.reshape(PREFIX_COUNT * PREFIX_PAGES, PAGE_TOKENS, KEY_VALUE_HEADS, HEAD_SIZE)[prefix_slot_map].reshape(PREFIX_COUNT, PREFIX_TOKENS, KEY_VALUE_HEADS, HEAD_SIZE)
    value_by_group = prefix_value_slots.reshape(PREFIX_COUNT * PREFIX_PAGES, PAGE_TOKENS, KEY_VALUE_HEADS, HEAD_SIZE)[prefix_slot_map].reshape(PREFIX_COUNT, PREFIX_TOKENS, KEY_VALUE_HEADS, HEAD_SIZE)

    def one_request(outputs, request_item):
        begin_page, page_count, group_id = request_item
        row_begin = (begin_page * PAGE_TOKENS).astype(jnp.int32)
        query_block_rows = lax.dynamic_slice_in_dim(padded_query, row_begin, sliding_window_rows, 0)
        block_key = lax.dynamic_slice_in_dim(key_with_padding, row_begin, sliding_window_rows, 0)
        block_value = lax.dynamic_slice_in_dim(value_with_padding, row_begin, sliding_window_rows, 0)
        group_keys = lax.dynamic_index_in_dim(key_by_group, group_id, 0, keepdims=False)
        group_values = lax.dynamic_index_in_dim(value_by_group, group_id, 0, keepdims=False)
        all_keys = jnp.concatenate([group_keys, block_key], axis=0).astype(jnp.float32)
        all_values = jnp.concatenate([group_values, block_value], axis=0).astype(jnp.float32)
        query_broadened = query_block_rows.astype(jnp.float32).reshape(sliding_window_rows, KEY_VALUE_HEADS, QUERY_HEADS // KEY_VALUE_HEADS, HEAD_SIZE)
        scores = jnp.einsum('qcgd,kcd->qcgk', query_broadened, all_keys)
        local_ids = jnp.arange(sliding_window_rows, dtype=jnp.int32)
        allowed = (local_ids[None, :] <= local_ids[:, None]) & (local_ids[None, :] < page_count * PAGE_TOKENS)
        allowed_keys = jnp.concatenate([jnp.ones((sliding_window_rows, PREFIX_TOKENS), bool), allowed], axis=1)[:, None, None, :]
        scores = jnp.where(allowed_keys, scores, masked_low)
        row_top = lax.optimization_barrier(jnp.max(scores, axis=-1, keepdims=True))
        weights = jnp.where(allowed_keys, jnp.exp(scores - row_top), 0.0)
        row_total = lax.optimization_barrier(jnp.sum(weights, axis=-1))
        rounded = lax.optimization_barrier(weights.astype(jnp.bfloat16)).astype(jnp.float32)
        mixture = jnp.einsum('qcgk,kcd->qcgd', rounded, all_values) / row_total[..., None]
        block_out = mixture.reshape(sliding_window_rows, QUERY_HEADS * HEAD_SIZE).astype(jnp.bfloat16)
        return (lax.dynamic_update_slice_in_dim(outputs, block_out, row_begin, 0), None)
    outputs = jnp.zeros((SUFFIX_TOKENS + sliding_window_rows, QUERY_HEADS * HEAD_SIZE), jnp.bfloat16)
    outputs, unused = lax.scan(one_request, outputs, (page_starts, page_lengths.astype(jnp.int32), request_group.astype(jnp.int32)))
    attended = outputs[:SUFFIX_TOKENS]
    attn_sum = jnp.dot(attended, w_out, preferred_element_type=jnp.float32)
    attn_branch = attn_sum * rms_scale(attn_sum) * post_gain
    low_rank = jnp.dot(normed, laurel_left, preferred_element_type=jnp.float32).astype(jnp.bfloat16)
    laurel_lr = jnp.dot(low_rank, laurel_right, preferred_element_type=jnp.float32)
    laurel = normed.astype(jnp.float32) + laurel_lr * rms_scale(laurel_lr) * laurel_gain
    layer_out = ((tokens.astype(jnp.float32) + attn_branch + laurel) * 2.0 ** (-0.5)).astype(jnp.bfloat16)
    paged_key_rows = fresh_key_rows.reshape(SUFFIX_PAGES, PAGE_TOKENS * KEY_VALUE_HEADS * HEAD_SIZE)
    paged_value_rows = fresh_value_rows.reshape(SUFFIX_PAGES, PAGE_TOKENS * KEY_VALUE_HEADS * HEAD_SIZE)
    suffix_key_cache = jnp.zeros_like(paged_key_rows).at[suffix_page_map].set(paged_key_rows).reshape(SUFFIX_TOKENS, KEY_VALUE_HEADS * HEAD_SIZE)
    suffix_value_cache = jnp.zeros_like(paged_value_rows).at[suffix_page_map].set(paged_value_rows).reshape(SUFFIX_TOKENS, KEY_VALUE_HEADS * HEAD_SIZE)
    return (layer_out, suffix_key_cache, suffix_value_cache)
```

```python
import functools

import jax
import jax.numpy as jnp
from jax import lax
from jax.experimental import pallas as pl
from jax.experimental.pallas import tpu as pltpu
from jax.sharding import PartitionSpec as P

HEAD_SIZE = 256
PAGE_TOKENS = 128
PREFIX_TOKENS = 4096
PREFIX_COUNT = 4
MAXP = 8
PREFIX_PAGES = 32


epsilon = 1e-06
rope_base = 1000000.0
masked_low = -1e30


PLANE = 4
CHUNK = 512
MESH = pl.DeviceIdType.MESH
ANY = pl.BlockSpec(memory_space=pl.ANY)
VMEM_LIMIT = 56 * 1024 * 1024


def rms_scale(values):
    return lax.rsqrt(jnp.mean(values * values, axis=-1, keepdims=True) + epsilon)


def rotate(values, positions):
    half_dim = values.shape[-1] // 2
    inv_freq = rope_base ** (-(jnp.arange(half_dim).astype(jnp.float32) * 2.0 / values.shape[-1]))
    angles = positions.astype(jnp.float32)[:, None] * inv_freq[None, :]
    cosine = jnp.cos(angles)[:, None, :]
    sines = jnp.sin(angles)[:, None, :]
    first_half = values[..., :half_dim]
    second_half = values[..., half_dim:]
    return jnp.concatenate(
        [first_half * cosine - second_half * sines, second_half * cosine + first_half * sines],
        axis=-1,
    )


def project(
    tokens,
    in_gain,
    w_query,
    key_projection_weight,
    value_projection_weight,
    q_gain,
    k_gain,
    positions,
):
    tok_count = tokens.shape[0]
    tokens_wide = tokens.astype(jnp.float32)
    normed = (tokens_wide * rms_scale(tokens_wide) * in_gain).astype(jnp.bfloat16)
    queries = jnp.dot(normed, w_query, preferred_element_type=jnp.float32).reshape(
        tok_count, -1, HEAD_SIZE
    )
    queries = rotate(queries * rms_scale(queries) * q_gain, positions).astype(jnp.bfloat16)
    fresh_key_rows = jnp.dot(
        normed, key_projection_weight, preferred_element_type=jnp.float32
    ).reshape(tok_count, -1, HEAD_SIZE)
    fresh_key_rows = rotate(fresh_key_rows * rms_scale(fresh_key_rows) * k_gain, positions).astype(
        jnp.bfloat16
    )
    fresh_value_rows = jnp.dot(
        normed, value_projection_weight, preferred_element_type=jnp.float32
    ).reshape(tok_count, -1, HEAD_SIZE)
    fresh_value_rows = (fresh_value_rows * rms_scale(fresh_value_rows)).astype(jnp.bfloat16)
    return (
        normed,
        queries,
        fresh_key_rows.reshape(tok_count, HEAD_SIZE),
        fresh_value_rows.reshape(tok_count, HEAD_SIZE),
    )


def greet(devices):
    barrier = pltpu.get_barrier_semaphore()
    for device in devices:
        pl.semaphore_signal(barrier, inc=1, device_id={"page": device}, device_id_type=MESH)
    pl.semaphore_wait(barrier, len(devices))


def gather_kernel(
    blocks, pk, pv, fk, fv, q, pk_all, pv_all, fk_all, fv_all, q_all, local_sem, send, recv, q_send, q_recv
):
    me = lax.axis_index("page")
    mine = lax.rem(me, PLANE)
    block = lax.div(me, PLANE)
    slot_x = mine + 1 - 2 * lax.rem(mine, 2)
    slot_y = lax.rem(mine + 2, PLANE)
    slot_far = slot_x + slot_y - mine
    base = block * PLANE
    peers = [lax.rem(block + d, blocks) * PLANE + mine for d in range(1, blocks)]
    greet([base + slot_x, base + slot_y, *peers])
    own = [(pk, pk_all), (fk, fk_all), (pv, pv_all), (fv, fv_all)]

    def copy(kind, source, slot, to, lane):
        return pltpu.make_async_remote_copy(
            src_ref=source,
            dst_ref=own[kind][1].at[slot],
            send_sem=send.at[kind, lane],
            recv_sem=recv.at[kind, slot],
            device_id={"page": base + to},
            device_id_type=MESH,
        )

    started = []

    def begin(made):
        made.start()
        started.append(made)

    for kind in (0, 1):
        begin(copy(kind, own[kind][0], mine, slot_x, 0))
    for kind in (2, 3):
        begin(copy(kind, own[kind][0], mine, slot_y, 1))
    arriving = []
    for d in range(1, blocks):
        to = lax.rem(block + d, blocks) * PLANE + mine
        begin(
            pltpu.make_async_remote_copy(
                src_ref=q,
                dst_ref=q_all.at[block],
                send_sem=q_send.at[d - 1],
                recv_sem=q_recv.at[d - 1],
                device_id={"page": to},
                device_id_type=MESH,
            )
        )
        arriving.append(
            pltpu.make_async_remote_copy(
                src_ref=q,
                dst_ref=q_all.at[lax.rem(block + blocks - d, blocks)],
                send_sem=q_send.at[d - 1],
                recv_sem=q_recv.at[d - 1],
                device_id={"page": to},
                device_id_type=MESH,
            )
        )
    for kind in (2, 3):
        begin(copy(kind, own[kind][0], mine, slot_x, 0))
    for kind in (0, 1):
        begin(copy(kind, own[kind][0], mine, slot_y, 1))
    locals_ = [
        pltpu.make_async_copy(source, whole.at[mine], local_sem.at[n])
        for n, (source, whole) in enumerate(own)
    ]
    locals_.append(pltpu.make_async_copy(q, q_all.at[block], local_sem.at[4]))
    for made in locals_:
        made.start()
    for kind in (0, 1, 2, 3):
        near, to, lane = (slot_x, slot_y, 2) if kind < 2 else (slot_y, slot_x, 2)
        copy(kind, own[kind][0], near, to, lane).wait_recv()
        begin(copy(kind, own[kind][1].at[near], near, to, lane))
    for kind in (0, 1, 2, 3):
        other = slot_y if kind < 2 else slot_x
        copy(kind, own[kind][0], other, other, 0).wait_recv()
        copy(kind, own[kind][0], slot_far, other, 0).wait_recv()
    for made in arriving:
        made.wait_recv()
    for made in started:
        made.wait_send()
    for made in locals_:
        made.wait()


def gather(pk, pv, fk, fv, q, blocks):
    def many(source, n):
        return jax.ShapeDtypeStruct((n, *source.shape), source.dtype)

    return pl.pallas_call(
        functools.partial(gather_kernel, blocks),
        out_shape=[many(pk, PLANE), many(pv, PLANE), many(fk, PLANE), many(fv, PLANE), many(q, blocks)],
        in_specs=[ANY] * 5,
        out_specs=[ANY] * 5,
        scratch_shapes=[
            pltpu.SemaphoreType.DMA((5,)),
            pltpu.SemaphoreType.DMA((4, 3)),
            pltpu.SemaphoreType.DMA((4, PLANE)),
            pltpu.SemaphoreType.DMA((blocks - 1,)),
            pltpu.SemaphoreType.DMA((blocks - 1,)),
        ],
        compiler_params=pltpu.CompilerParams(collective_id=0, has_side_effects=True),
    )(pk, pv, fk, fv, q)


def attend_kernel(
    slots, places, info, pk, pv, fk, fv, q_ref, out_ref, stat_ref, keys, values, top, total, mixed, sem
):
    step = pl.program_id(0)
    prefix_rows = slots * PAGE_TOKENS
    suffix_rows = fk.shape[0]

    @pl.when(step == 0)
    def _():
        values[prefix_rows + suffix_rows :, :] = jnp.zeros((CHUNK, HEAD_SIZE), jnp.bfloat16)
        moves = [
            pltpu.make_async_copy(fk, keys.at[pl.ds(prefix_rows, suffix_rows), :], sem.at[2 * slots]),
            pltpu.make_async_copy(
                fv, values.at[pl.ds(prefix_rows, suffix_rows), :], sem.at[2 * slots + 1]
            ),
        ]
        for n in range(slots):
            source = pl.ds(n * PAGE_TOKENS, PAGE_TOKENS)
            there = pl.ds(pl.multiple_of(places[n] * PAGE_TOKENS, PAGE_TOKENS), PAGE_TOKENS)
            moves.append(pltpu.make_async_copy(pk.at[source, :], keys.at[there, :], sem.at[n]))
            moves.append(
                pltpu.make_async_copy(pv.at[source, :], values.at[there, :], sem.at[slots + n])
            )
        for move in moves:
            move.start()
        for move in moves:
            move.wait()

    top[...] = jnp.full_like(top, masked_low)
    total[...] = jnp.zeros_like(total)
    mixed[...] = jnp.zeros_like(mixed)
    rows = q_ref.shape[1]
    prefix_low, prefix_high = info[step * 8], info[step * 8 + 1]
    suffix_low, suffix_high = info[step * 8 + 2], info[step * 8 + 3]
    first_token = info[step * 8 + 4]

    def fold(offset, valid):
        offset = pl.multiple_of(offset, PAGE_TOKENS)
        scores = lax.dot_general(
            keys[pl.ds(offset, CHUNK), :],
            q_ref[0],
            (((1,), (1,)), ((), ())),
            preferred_element_type=jnp.float32,
        )
        scores = jnp.where(valid, scores, masked_low)
        row_top = jnp.maximum(top[...], jnp.max(scores, axis=0, keepdims=True))
        factor = jnp.exp(top[...] - row_top)
        weights = jnp.exp(scores - row_top)
        total[...] = total[...] * factor + jnp.sum(weights, axis=0, keepdims=True)
        mixed[...] = mixed[...] * factor + lax.dot_general(
            values[pl.ds(offset, CHUNK), :],
            weights.astype(jnp.bfloat16),
            (((0,), (0,)), ((), ())),
            preferred_element_type=jnp.float32,
        )
        top[...] = row_top

    in_chunk = lax.broadcasted_iota(jnp.int32, (CHUNK, rows), 0)
    token = lax.rem(lax.broadcasted_iota(jnp.int32, (CHUNK, rows), 1), PAGE_TOKENS)
    chunk_pages = CHUNK // PAGE_TOKENS

    def prefix_step(n, _):
        start = (prefix_low + n * chunk_pages) * PAGE_TOKENS
        fold(start, in_chunk < prefix_high * PAGE_TOKENS - start)
        return 0

    def suffix_step(n, _):
        start = (suffix_low + n * chunk_pages) * PAGE_TOKENS
        valid = (in_chunk < suffix_high * PAGE_TOKENS - start) & (
            in_chunk - token <= first_token - start
        )
        fold(start + prefix_rows, valid)
        return 0

    lax.fori_loop(0, lax.div(prefix_high - prefix_low + chunk_pages - 1, chunk_pages), prefix_step, 0)
    lax.fori_loop(0, lax.div(suffix_high - suffix_low + chunk_pages - 1, chunk_pages), suffix_step, 0)
    scale = jnp.where(total[...] > 0, 1.0 / jnp.maximum(total[...], 1e-30), 0.0)
    out_ref[0] = (mixed[...] * scale).astype(jnp.bfloat16)
    stat_ref[0, 0:1, :] = top[...]
    stat_ref[0, 1:2, :] = total[...]
    stat_ref[0, 2:8, :] = jnp.zeros((6, rows), jnp.float32)


def attend(places, info, pk, pv, fk, fv, queries):
    pages, rows, _ = queries.shape
    slots = places.shape[0]
    span = pk.shape[0] + fk.shape[0] + CHUNK
    return pl.pallas_call(
        functools.partial(attend_kernel, slots),
        out_shape=[
            jax.ShapeDtypeStruct((pages, HEAD_SIZE, rows), jnp.bfloat16),
            jax.ShapeDtypeStruct((pages, 8, rows), jnp.float32),
        ],
        grid_spec=pltpu.PrefetchScalarGridSpec(
            num_scalar_prefetch=2,
            grid=(pages,),
            in_specs=[ANY] * 4 + [pl.BlockSpec((1, rows, HEAD_SIZE), lambda i, *_: (i, 0, 0))],
            out_specs=[
                pl.BlockSpec((1, HEAD_SIZE, rows), lambda i, *_: (i, 0, 0)),
                pl.BlockSpec((1, 8, rows), lambda i, *_: (i, 0, 0)),
            ],
            scratch_shapes=[
                pltpu.VMEM((span, HEAD_SIZE), jnp.bfloat16),
                pltpu.VMEM((span, HEAD_SIZE), jnp.bfloat16),
                pltpu.VMEM((1, rows), jnp.float32),
                pltpu.VMEM((1, rows), jnp.float32),
                pltpu.VMEM((HEAD_SIZE, rows), jnp.float32),
                pltpu.SemaphoreType.DMA((2 * slots + 2,)),
            ],
        ),
        compiler_params=pltpu.CompilerParams(vmem_limit_bytes=VMEM_LIMIT),
    )(places, info, pk, pv, fk, fv, queries)


def send_back_kernel(blocks, out, stat, out_all, stat_all, local_sem, send, recv):
    me = lax.axis_index("page")
    mine = lax.rem(me, PLANE)
    block = lax.div(me, PLANE)
    greet([lax.rem(block + d, blocks) * PLANE + mine for d in range(1, blocks)])
    started = []
    arriving = []
    for d in range(1, blocks):
        other = lax.rem(block + d, blocks)
        for n, (source, whole) in enumerate(((out, out_all), (stat, stat_all))):
            for slot, made in ((block, started), (lax.rem(block + blocks - d, blocks), arriving)):
                made.append(
                    pltpu.make_async_remote_copy(
                        src_ref=source.at[other],
                        dst_ref=whole.at[slot],
                        send_sem=send.at[n, d - 1],
                        recv_sem=recv.at[n, d - 1],
                        device_id={"page": other * PLANE + mine},
                        device_id_type=MESH,
                    )
                )
            started[-1].start()
    own = [
        pltpu.make_async_copy(out.at[block], out_all.at[block], local_sem.at[0]),
        pltpu.make_async_copy(stat.at[block], stat_all.at[block], local_sem.at[1]),
    ]
    for made in own:
        made.start()
    for made in arriving:
        made.wait_recv()
    for made in started:
        made.wait_send()
    for made in own:
        made.wait()


def send_back(out, stat):
    blocks = out.shape[0]
    return pl.pallas_call(
        functools.partial(send_back_kernel, blocks),
        out_shape=[
            jax.ShapeDtypeStruct(out.shape, out.dtype),
            jax.ShapeDtypeStruct(stat.shape, stat.dtype),
        ],
        in_specs=[ANY] * 2,
        out_specs=[ANY] * 2,
        scratch_shapes=[
            pltpu.SemaphoreType.DMA((2,)),
            pltpu.SemaphoreType.DMA((2, blocks - 1)),
            pltpu.SemaphoreType.DMA((2, blocks - 1)),
        ],
        compiler_params=pltpu.CompilerParams(collective_id=1, has_side_effects=True),
    )(out, stat)


def page_facts(pages, page_lengths, request_group):
    ids = jnp.arange(page_lengths.shape[0])
    starts = jnp.sum(jnp.where(ids[None, :] < ids[:, None], page_lengths[None, :], 0), axis=1)
    belongs = (pages[:, None] >= starts[None, :]) & (
        pages[:, None] < (starts + page_lengths)[None, :]
    )
    first = jnp.sum(jnp.where(belongs, starts[None, :], 0), axis=1)
    group = jnp.sum(jnp.where(belongs, request_group[None, :], 0), axis=1)
    return first, group


def local(
    tokens,
    in_gain,
    w_query,
    key_projection_weight,
    value_projection_weight,
    q_gain,
    k_gain,
    w_out,
    post_gain,
    laurel_left,
    laurel_right,
    laurel_gain,
    prefix_key_slots,
    prefix_value_slots,
    prefix_slot_map,
    page_lengths,
    request_group,
    suffix_page_map,
):
    tok_count, model_width = tokens.shape
    pages_here = tok_count // PAGE_TOKENS
    device = lax.axis_index("page")
    blocks = lax.axis_size("page") // PLANE
    mine = device % PLANE
    block = device // PLANE
    heads = w_query.shape[1] // HEAD_SIZE
    plane_pages = PLANE * pages_here

    my_pages = device * pages_here + jnp.arange(pages_here, dtype=jnp.int32)
    my_first, _ = page_facts(my_pages, page_lengths, request_group)
    position = (
        (my_pages - my_first)[:, None] * PAGE_TOKENS + jnp.arange(PAGE_TOKENS, dtype=jnp.int32)
    ).reshape(tok_count)
    normed, queries, fresh_key_rows, fresh_value_rows = project(
        tokens,
        in_gain,
        w_query,
        key_projection_weight,
        value_projection_weight,
        q_gain,
        k_gain,
        position + PREFIX_TOKENS,
    )
    local_slot = suffix_page_map - device * pages_here

    def place(rows):
        paged = rows.reshape(pages_here, PAGE_TOKENS, HEAD_SIZE)
        parts = []
        for slot in range(pages_here):
            part = paged[0]
            for n in range(1, pages_here):
                part = jnp.where(local_slot[n] == slot, paged[n], part)
            parts.append(part)
        return jnp.concatenate(parts, axis=0)

    suffix_key_cache = place(fresh_key_rows)
    suffix_value_cache = place(fresh_value_rows)

    slots = PLANE * prefix_key_slots.shape[0] // PAGE_TOKENS
    slot_ids = block * slots + jnp.arange(slots, dtype=jnp.int32)
    map_group = jnp.arange(prefix_slot_map.shape[0], dtype=jnp.int32) // PREFIX_PAGES
    slot_group = jnp.sum(
        jnp.where(slot_ids[:, None] == prefix_slot_map[None, :], map_group[None, :], 0), axis=1
    )
    order = jnp.arange(slots, dtype=jnp.int32)
    ahead = (slot_group[None, :] < slot_group[:, None]) | (
        (slot_group[None, :] == slot_group[:, None]) & (order[None, :] < order[:, None])
    )
    places = jnp.sum(ahead.astype(jnp.int32), axis=1)
    q_pages = (
        (jnp.arange(blocks, dtype=jnp.int32) * PLANE + mine)[:, None] * pages_here
        + jnp.arange(pages_here, dtype=jnp.int32)
    ).reshape(-1)
    q_first, q_group = page_facts(q_pages, page_lengths, request_group)
    prefix_low = jnp.sum((slot_group[None, :] < q_group[:, None]).astype(jnp.int32), axis=1)
    prefix_high = jnp.sum((slot_group[None, :] <= q_group[:, None]).astype(jnp.int32), axis=1)
    plane_first = block * plane_pages
    suffix_low = jnp.maximum(q_first - plane_first, 0)
    suffix_high = jnp.minimum(q_pages + 1 - plane_first, plane_pages)
    suffix_low = jnp.minimum(suffix_low, plane_pages)
    suffix_high = jnp.maximum(suffix_high, suffix_low)
    first_token = (q_pages - plane_first) * PAGE_TOKENS
    nothing = jnp.zeros_like(first_token)
    info = jnp.stack(
        [prefix_low, prefix_high, suffix_low, suffix_high, first_token, nothing, nothing, nothing],
        axis=1,
    ).reshape(-1)

    paged_queries = queries.reshape(pages_here, PAGE_TOKENS, heads, HEAD_SIZE).transpose(0, 2, 1, 3)
    paged_queries = paged_queries.reshape(pages_here * heads * PAGE_TOKENS, HEAD_SIZE)
    pk, pv, fk, fv, q_all = gather(
        prefix_key_slots, prefix_value_slots, fresh_key_rows, fresh_value_rows, paged_queries, blocks
    )
    out, stat = attend(
        places,
        info,
        pk.reshape(-1, HEAD_SIZE),
        pv.reshape(-1, HEAD_SIZE),
        fk.reshape(-1, HEAD_SIZE),
        fv.reshape(-1, HEAD_SIZE),
        q_all.reshape(blocks * pages_here, heads * PAGE_TOKENS, HEAD_SIZE),
    )
    out, stat = send_back(
        out.reshape(blocks, pages_here, HEAD_SIZE, -1), stat.reshape(blocks, pages_here, 8, -1)
    )
    tops, totals = stat[:, :, 0, :], stat[:, :, 1, :]
    share = totals * jnp.exp(tops - jnp.max(tops, axis=0, keepdims=True))
    share = share / jnp.sum(share, axis=0, keepdims=True)
    attended = jnp.sum(out.astype(jnp.float32) * share[:, :, None, :], axis=0).astype(jnp.bfloat16)
    attended = (
        attended.reshape(pages_here, HEAD_SIZE, heads, PAGE_TOKENS)
        .transpose(0, 3, 2, 1)
        .reshape(tok_count, heads * HEAD_SIZE)
    )
    attn_part = jnp.dot(attended, w_out, preferred_element_type=jnp.float32).astype(jnp.bfloat16)
    other_part = lax.ppermute(attn_part, "kv", [(0, 1), (1, 0)])
    summed_out = attn_part.astype(jnp.float32) + other_part.astype(jnp.float32)
    kv_index = lax.axis_index("kv")
    half_width = model_width // lax.axis_size("kv")

    def columns(source):
        return lax.dynamic_slice_in_dim(source, kv_index * half_width, half_width, source.ndim - 1)

    low_rank = jnp.dot(normed, laurel_left, preferred_element_type=jnp.float32).astype(jnp.bfloat16)
    laurel_full = jnp.dot(low_rank, laurel_right, preferred_element_type=jnp.float32)
    laurel_part = columns(laurel_full) * rms_scale(laurel_full) * columns(laurel_gain)
    laurel = columns(normed).astype(jnp.float32) + laurel_part
    attn_branch = columns(summed_out) * rms_scale(summed_out) * columns(post_gain)
    layer_out = (
        (columns(tokens).astype(jnp.float32) + attn_branch + laurel) * 2.0 ** (-0.5)
    ).astype(jnp.bfloat16)
    return (layer_out, suffix_key_cache, suffix_value_cache)


def solution(mesh):
    placed = (
        P("page", None),
        P(),
        P(None, "kv"),
        P(None, "kv"),
        P(None, "kv"),
        P(),
        P(),
        P("kv", None),
        P(),
        P(),
        P(),
        P(),
        P("page", "kv"),
        P("page", "kv"),
        P(),
        P(),
        P(),
        P("page"),
    )
    return jax.shard_map(
        local,
        mesh=mesh,
        in_specs=placed,
        out_specs=(P("page", "kv"), P("page", "kv"), P("page", "kv")),
        check_vma=False,
    )
```

```python
import functools

import jax
import jax.numpy as jnp
from jax import lax
from jax.experimental import pallas as pl
from jax.experimental.pallas import tpu as pltpu
from jax.sharding import PartitionSpec as P

HEAD_SIZE = 256
PAGE_TOKENS = 128
PREFIX_TOKENS = 4096
PREFIX_COUNT = 4
MAXP = 8
PREFIX_PAGES = 32


epsilon = 1e-06
rope_base = 1000000.0
masked_low = -1e30


PLANE = 4
CHUNK = 512
MESH = pl.DeviceIdType.MESH
ANY = pl.BlockSpec(memory_space=pl.ANY)
VMEM_LIMIT = 56 * 1024 * 1024


def rms_scale(values):
    return lax.rsqrt(jnp.mean(values * values, axis=-1, keepdims=True) + epsilon)


def rotate(values, positions):
    half_dim = values.shape[-1] // 2
    inv_freq = rope_base ** (-(jnp.arange(half_dim).astype(jnp.float32) * 2.0 / values.shape[-1]))
    angles = positions.astype(jnp.float32)[:, None] * inv_freq[None, :]
    cosine = jnp.cos(angles)[:, None, :]
    sines = jnp.sin(angles)[:, None, :]
    first_half = values[..., :half_dim]
    second_half = values[..., half_dim:]
    return jnp.concatenate(
        [first_half * cosine - second_half * sines, second_half * cosine + first_half * sines],
        axis=-1,
    )


def project(
    tokens,
    in_gain,
    w_query,
    key_projection_weight,
    value_projection_weight,
    q_gain,
    k_gain,
    positions,
):
    tok_count = tokens.shape[0]
    tokens_wide = tokens.astype(jnp.float32)
    normed = (tokens_wide * rms_scale(tokens_wide) * in_gain).astype(jnp.bfloat16)
    queries = jnp.dot(normed, w_query, preferred_element_type=jnp.float32).reshape(
        tok_count, -1, HEAD_SIZE
    )
    queries = rotate(queries * rms_scale(queries) * q_gain, positions).astype(jnp.bfloat16)
    fresh_key_rows = jnp.dot(
        normed, key_projection_weight, preferred_element_type=jnp.float32
    ).reshape(tok_count, -1, HEAD_SIZE)
    fresh_key_rows = rotate(fresh_key_rows * rms_scale(fresh_key_rows) * k_gain, positions).astype(
        jnp.bfloat16
    )
    fresh_value_rows = jnp.dot(
        normed, value_projection_weight, preferred_element_type=jnp.float32
    ).reshape(tok_count, -1, HEAD_SIZE)
    fresh_value_rows = (fresh_value_rows * rms_scale(fresh_value_rows)).astype(jnp.bfloat16)
    return (
        normed,
        queries,
        fresh_key_rows.reshape(tok_count, HEAD_SIZE),
        fresh_value_rows.reshape(tok_count, HEAD_SIZE),
    )


def greet(devices):
    barrier = pltpu.get_barrier_semaphore()
    for device in devices:
        pl.semaphore_signal(barrier, inc=1, device_id={"page": device}, device_id_type=MESH)
    pl.semaphore_wait(barrier, len(devices))


def gather_kernel(blocks, fresh, q, fresh_all, q_all, local_sem, send, recv, q_send, q_recv):
    me = lax.axis_index("page")
    mine = lax.rem(me, PLANE)
    block = lax.div(me, PLANE)
    base = block * PLANE
    z_peers = [lax.rem(block + d, blocks) * PLANE + mine for d in range(1, blocks)]
    peers = [base + lax.rem(mine + d, PLANE) for d in range(1, PLANE)]
    greet([*z_peers, *peers])
    started = []
    for d in range(1, blocks):
        started.append(
            pltpu.make_async_remote_copy(
                src_ref=q,
                dst_ref=q_all.at[d],
                send_sem=q_send.at[d - 1],
                recv_sem=q_recv.at[d - 1],
                device_id={"page": z_peers[d - 1]},
                device_id_type=MESH,
            )
        )
        started[-1].start()
    for d in range(1, PLANE):
        made = pltpu.make_async_remote_copy(
            src_ref=fresh,
            dst_ref=fresh_all.at[mine],
            send_sem=send.at[d - 1],
            recv_sem=recv.at[d - 1],
            device_id={"page": peers[d - 1]},
            device_id_type=MESH,
        )
        made.start()
        started.append(made)
    own = [
        pltpu.make_async_copy(fresh, fresh_all.at[mine], local_sem.at[0]),
        pltpu.make_async_copy(q, q_all.at[0], local_sem.at[1]),
    ]
    for made in own:
        made.start()
    for made in started[: blocks - 1]:
        made.wait_recv()
    for d in range(1, PLANE):
        pltpu.make_async_remote_copy(
            src_ref=fresh,
            dst_ref=fresh_all.at[lax.rem(mine + PLANE - d, PLANE)],
            send_sem=send.at[d - 1],
            recv_sem=recv.at[d - 1],
            device_id={"page": peers[d - 1]},
            device_id_type=MESH,
        ).wait_recv()
    for made in started:
        made.wait_send()
    for made in own:
        made.wait()


def gather(fresh, q, blocks):
    return pl.pallas_call(
        functools.partial(gather_kernel, blocks),
        out_shape=[
            jax.ShapeDtypeStruct((PLANE, *fresh.shape), fresh.dtype),
            jax.ShapeDtypeStruct((blocks, *q.shape), q.dtype),
        ],
        in_specs=[ANY] * 2,
        out_specs=[ANY] * 2,
        scratch_shapes=[
            pltpu.SemaphoreType.DMA((2,)),
            pltpu.SemaphoreType.DMA((PLANE - 1,)),
            pltpu.SemaphoreType.DMA((PLANE - 1,)),
            pltpu.SemaphoreType.DMA((blocks - 1,)),
            pltpu.SemaphoreType.DMA((blocks - 1,)),
        ],
        compiler_params=pltpu.CompilerParams(collective_id=0, has_side_effects=True),
        cost_estimate=pl.CostEstimate(flops=40 * 10**9, bytes_accessed=10**6, transcendentals=0),
    )(fresh, q)


def attend_kernel(
    slots, first, places, info, *refs
):
    parts = refs[:PLANE]
    fresh, q_ref, out_ref, stat_ref, keys, values, top, total, mixed, sem = refs[-10:]
    step = pl.program_id(0)
    prefix_rows = slots * PAGE_TOKENS
    part_rows = fresh.shape[2]
    suffix_rows = PLANE * part_rows
    part_slots = slots // PLANE
    entry = (first + step) * 8

    @pl.when(step == 0)
    def _():
        values[prefix_rows + suffix_rows :, :] = jnp.zeros((CHUNK, HEAD_SIZE), jnp.bfloat16)
        moves = []
        for n in range(PLANE):
            for which, whole in enumerate((keys, values)):
                there = pl.ds(prefix_rows + n * part_rows, part_rows)
                moves.append((fresh.at[n, which], whole.at[there, :]))
        for n in range(slots):
            source = pl.ds((n % part_slots) * PAGE_TOKENS, PAGE_TOKENS)
            there = pl.ds(pl.multiple_of(places[n] * PAGE_TOKENS, PAGE_TOKENS), PAGE_TOKENS)
            for which, whole in enumerate((keys, values)):
                moves.append((parts[n // part_slots].at[which, source, :], whole.at[there, :]))
        moves = [pltpu.make_async_copy(*move, sem.at[n]) for n, move in enumerate(moves)]
        for move in moves:
            move.start()
        for move in moves:
            move.wait()

    top[...] = jnp.full_like(top, masked_low)
    total[...] = jnp.zeros_like(total)
    mixed[...] = jnp.zeros_like(mixed)
    rows = q_ref.shape[1]
    prefix_low, prefix_high = info[entry], info[entry + 1]
    suffix_low, suffix_high = info[entry + 2], info[entry + 3]
    first_token = info[entry + 4]

    def fold(offset, valid):
        offset = pl.multiple_of(offset, PAGE_TOKENS)
        scores = lax.dot_general(
            keys[pl.ds(offset, CHUNK), :],
            q_ref[0],
            (((1,), (1,)), ((), ())),
            preferred_element_type=jnp.float32,
        )
        scores = jnp.where(valid, scores, masked_low)
        row_top = jnp.maximum(top[...], jnp.max(scores, axis=0, keepdims=True))
        factor = jnp.exp(top[...] - row_top)
        weights = jnp.exp(scores - row_top)
        total[...] = total[...] * factor + jnp.sum(weights, axis=0, keepdims=True)
        mixed[...] = mixed[...] * factor + lax.dot_general(
            values[pl.ds(offset, CHUNK), :],
            weights.astype(jnp.bfloat16),
            (((0,), (0,)), ((), ())),
            preferred_element_type=jnp.float32,
        )
        top[...] = row_top

    in_chunk = lax.broadcasted_iota(jnp.int32, (CHUNK, rows), 0)
    token = lax.rem(lax.broadcasted_iota(jnp.int32, (CHUNK, rows), 1), PAGE_TOKENS)
    chunk_pages = CHUNK // PAGE_TOKENS

    def prefix_step(n, _):
        start = (prefix_low + n * chunk_pages) * PAGE_TOKENS
        fold(start, in_chunk < prefix_high * PAGE_TOKENS - start)
        return 0

    def suffix_step(n, _):
        start = (suffix_low + n * chunk_pages) * PAGE_TOKENS
        valid = (in_chunk < suffix_high * PAGE_TOKENS - start) & (
            in_chunk - token <= first_token - start
        )
        fold(start + prefix_rows, valid)
        return 0

    lax.fori_loop(0, lax.div(prefix_high - prefix_low + chunk_pages - 1, chunk_pages), prefix_step, 0)
    lax.fori_loop(0, lax.div(suffix_high - suffix_low + chunk_pages - 1, chunk_pages), suffix_step, 0)
    scale = jnp.where(total[...] > 0, 1.0 / jnp.maximum(total[...], 1e-30), 0.0)
    out_ref[0] = (mixed[...] * scale).astype(jnp.bfloat16)
    stat_ref[0, 0:1, :] = top[...]
    stat_ref[0, 1:2, :] = total[...]
    stat_ref[0, 2:8, :] = jnp.zeros((6, rows), jnp.float32)


def attend(places, info, parts, fresh, after, queries, first, pages):
    _, rows, _ = queries.shape
    slots = places.shape[0]
    span = (slots * PAGE_TOKENS) + PLANE * fresh.shape[2] + CHUNK
    return pl.pallas_call(
        functools.partial(attend_kernel, slots, first),
        out_shape=[
            jax.ShapeDtypeStruct((pages, HEAD_SIZE, rows), jnp.bfloat16),
            jax.ShapeDtypeStruct((pages, 8, rows), jnp.float32),
        ],
        grid_spec=pltpu.PrefetchScalarGridSpec(
            num_scalar_prefetch=2,
            grid=(pages,),
            in_specs=[ANY] * (PLANE + 1 + len(after))
            + [pl.BlockSpec((1, rows, HEAD_SIZE), lambda i, *_: (first + i, 0, 0))],
            out_specs=[
                pl.BlockSpec((1, HEAD_SIZE, rows), lambda i, *_: (i, 0, 0)),
                pl.BlockSpec((1, 8, rows), lambda i, *_: (i, 0, 0)),
            ],
            scratch_shapes=[
                pltpu.VMEM((span, HEAD_SIZE), jnp.bfloat16),
                pltpu.VMEM((span, HEAD_SIZE), jnp.bfloat16),
                pltpu.VMEM((1, rows), jnp.float32),
                pltpu.VMEM((1, rows), jnp.float32),
                pltpu.VMEM((HEAD_SIZE, rows), jnp.float32),
                pltpu.SemaphoreType.DMA((2 * slots + 2 * PLANE,)),
            ],
        ),
        compiler_params=pltpu.CompilerParams(vmem_limit_bytes=VMEM_LIMIT),
        cost_estimate=pl.CostEstimate(
            flops=10**8, bytes_accessed=10**5, transcendentals=0
        ),
    )(places, info, *parts, *after, fresh, queries)


def moved(block, axis_size, target):
    return lax.ppermute(block, "page", [(p, target(p)) for p in range(axis_size)])


def page_facts(pages, page_lengths, request_group):
    ids = jnp.arange(page_lengths.shape[0])
    starts = jnp.sum(jnp.where(ids[None, :] < ids[:, None], page_lengths[None, :], 0), axis=1)
    belongs = (pages[:, None] >= starts[None, :]) & (
        pages[:, None] < (starts + page_lengths)[None, :]
    )
    first = jnp.sum(jnp.where(belongs, starts[None, :], 0), axis=1)
    group = jnp.sum(jnp.where(belongs, request_group[None, :], 0), axis=1)
    return first, group


def local(
    tokens,
    in_gain,
    w_query,
    key_projection_weight,
    value_projection_weight,
    q_gain,
    k_gain,
    w_out,
    post_gain,
    laurel_left,
    laurel_right,
    laurel_gain,
    prefix_key_slots,
    prefix_value_slots,
    prefix_slot_map,
    page_lengths,
    request_group,
    suffix_page_map,
):
    tok_count, model_width = tokens.shape
    pages_here = tok_count // PAGE_TOKENS
    device = lax.axis_index("page")
    blocks = lax.axis_size("page") // PLANE
    mine = device % PLANE
    block = device // PLANE
    heads = w_query.shape[1] // HEAD_SIZE
    plane_pages = PLANE * pages_here

    my_pages = device * pages_here + jnp.arange(pages_here, dtype=jnp.int32)
    my_first, _ = page_facts(my_pages, page_lengths, request_group)
    position = (
        (my_pages - my_first)[:, None] * PAGE_TOKENS + jnp.arange(PAGE_TOKENS, dtype=jnp.int32)
    ).reshape(tok_count)
    normed, queries, fresh_key_rows, fresh_value_rows = project(
        tokens,
        in_gain,
        w_query,
        key_projection_weight,
        value_projection_weight,
        q_gain,
        k_gain,
        position + PREFIX_TOKENS,
    )
    local_slot = suffix_page_map - device * pages_here

    def place(rows):
        paged = rows.reshape(pages_here, PAGE_TOKENS, HEAD_SIZE)
        parts = []
        for slot in range(pages_here):
            part = paged[0]
            for n in range(1, pages_here):
                part = jnp.where(local_slot[n] == slot, paged[n], part)
            parts.append(part)
        return jnp.concatenate(parts, axis=0)

    suffix_key_cache = place(fresh_key_rows)
    suffix_value_cache = place(fresh_value_rows)

    slots = PLANE * prefix_key_slots.shape[0] // PAGE_TOKENS
    part_slots = slots // PLANE
    slot_parts = jnp.arange(slots, dtype=jnp.int32) // part_slots
    slot_ids = (block * PLANE + (mine ^ slot_parts)) * part_slots + jnp.arange(
        slots, dtype=jnp.int32
    ) % part_slots
    map_group = jnp.arange(prefix_slot_map.shape[0], dtype=jnp.int32) // PREFIX_PAGES
    slot_group = jnp.sum(
        jnp.where(slot_ids[:, None] == prefix_slot_map[None, :], map_group[None, :], 0), axis=1
    )
    order = jnp.arange(slots, dtype=jnp.int32)
    ahead = (slot_group[None, :] < slot_group[:, None]) | (
        (slot_group[None, :] == slot_group[:, None]) & (order[None, :] < order[:, None])
    )
    places = jnp.sum(ahead.astype(jnp.int32), axis=1)
    q_pages = (
        ((block + blocks - jnp.arange(blocks, dtype=jnp.int32)) % blocks * PLANE + mine)[:, None]
        * pages_here
        + jnp.arange(pages_here, dtype=jnp.int32)
    ).reshape(-1)
    q_first, q_group = page_facts(q_pages, page_lengths, request_group)
    prefix_low = jnp.sum((slot_group[None, :] < q_group[:, None]).astype(jnp.int32), axis=1)
    prefix_high = jnp.sum((slot_group[None, :] <= q_group[:, None]).astype(jnp.int32), axis=1)
    plane_first = block * plane_pages
    suffix_low = jnp.maximum(q_first - plane_first, 0)
    suffix_high = jnp.minimum(q_pages + 1 - plane_first, plane_pages)
    suffix_low = jnp.minimum(suffix_low, plane_pages)
    suffix_high = jnp.maximum(suffix_high, suffix_low)
    first_token = (q_pages - plane_first) * PAGE_TOKENS
    nothing = jnp.zeros_like(first_token)
    info = jnp.stack(
        [prefix_low, prefix_high, suffix_low, suffix_high, first_token, nothing, nothing, nothing],
        axis=1,
    ).reshape(-1)

    paged_queries = queries.reshape(pages_here, PAGE_TOKENS, heads, HEAD_SIZE).transpose(0, 2, 1, 3)
    paged_queries = paged_queries.reshape(pages_here * heads * PAGE_TOKENS, HEAD_SIZE)
    size = lax.axis_size("page")
    prefix = jnp.stack([prefix_key_slots, prefix_value_slots])
    parts = (
        prefix,
        moved(prefix, size, lambda p: p ^ 1),
        moved(prefix, size, lambda p: p ^ 2),
        moved(prefix, size, lambda p: p ^ 3),
    )
    fresh, q_all = gather(jnp.stack([fresh_key_rows, fresh_value_rows]), paged_queries, blocks)
    q_all = q_all.reshape(blocks * pages_here, heads * PAGE_TOKENS, HEAD_SIZE)
    outs, stats = [], []
    for d in [*range(1, blocks), 0]:
        out, stat = attend(
            places, info, parts, fresh, outs[-2:-1], q_all, d * pages_here, pages_here
        )
        if d:
            back = lambda p, d=d: (p // PLANE + blocks - d) % blocks * PLANE + p % PLANE
            out, stat = moved(out, size, back), moved(stat, size, back)
        outs.append(out)
        stats.append(stat)
    out, stat = jnp.stack(outs), jnp.stack(stats)
    tops, totals = stat[:, :, 0, :], stat[:, :, 1, :]
    share = totals * jnp.exp(tops - jnp.max(tops, axis=0, keepdims=True))
    share = share / jnp.sum(share, axis=0, keepdims=True)
    attended = jnp.sum(out.astype(jnp.float32) * share[:, :, None, :], axis=0).astype(jnp.bfloat16)
    attended = (
        attended.reshape(pages_here, HEAD_SIZE, heads, PAGE_TOKENS)
        .transpose(0, 3, 2, 1)
        .reshape(tok_count, heads * HEAD_SIZE)
    )
    attn_part = jnp.dot(attended, w_out, preferred_element_type=jnp.float32).astype(jnp.bfloat16)
    other_part = lax.ppermute(attn_part, "kv", [(0, 1), (1, 0)])
    summed_out = attn_part.astype(jnp.float32) + other_part.astype(jnp.float32)
    kv_index = lax.axis_index("kv")
    half_width = model_width // lax.axis_size("kv")

    def columns(source):
        return lax.dynamic_slice_in_dim(source, kv_index * half_width, half_width, source.ndim - 1)

    low_rank = jnp.dot(normed, laurel_left, preferred_element_type=jnp.float32).astype(jnp.bfloat16)
    laurel_full = jnp.dot(low_rank, laurel_right, preferred_element_type=jnp.float32)
    laurel_part = columns(laurel_full) * rms_scale(laurel_full) * columns(laurel_gain)
    laurel = columns(normed).astype(jnp.float32) + laurel_part
    attn_branch = columns(summed_out) * rms_scale(summed_out) * columns(post_gain)
    layer_out = (
        (columns(tokens).astype(jnp.float32) + attn_branch + laurel) * 2.0 ** (-0.5)
    ).astype(jnp.bfloat16)
    return (layer_out, suffix_key_cache, suffix_value_cache)


def solution(mesh):
    placed = (
        P("page", None),
        P(),
        P(None, "kv"),
        P(None, "kv"),
        P(None, "kv"),
        P(),
        P(),
        P("kv", None),
        P(),
        P(),
        P(),
        P(),
        P("page", "kv"),
        P("page", "kv"),
        P(),
        P(),
        P(),
        P("page"),
    )
    return jax.shard_map(
        local,
        mesh=mesh,
        in_specs=placed,
        out_specs=(P("page", "kv"), P("page", "kv"), P("page", "kv")),
        check_vma=False,
    )
```

```python
import functools

import jax
import jax.numpy as jnp
from jax import lax
from jax.experimental import pallas as pl
from jax.experimental.pallas import tpu as pltpu
from jax.sharding import PartitionSpec as P

HEAD_SIZE = 256
PAGE_TOKENS = 128
PREFIX_TOKENS = 4096
PREFIX_COUNT = 4
MAXP = 8
PREFIX_PAGES = 32


epsilon = 1e-06
rope_base = 1000000.0
masked_low = -1e30


PLANE = 4
CHUNK = 512
MESH = pl.DeviceIdType.MESH
ANY = pl.BlockSpec(memory_space=pl.ANY)
VMEM_LIMIT = 56 * 1024 * 1024


def rms_scale(values):
    return lax.rsqrt(jnp.mean(values * values, axis=-1, keepdims=True) + epsilon)


def rotate(values, positions):
    half_dim = values.shape[-1] // 2
    inv_freq = rope_base ** (-(jnp.arange(half_dim).astype(jnp.float32) * 2.0 / values.shape[-1]))
    angles = positions.astype(jnp.float32)[:, None] * inv_freq[None, :]
    cosine = jnp.cos(angles)[:, None, :]
    sines = jnp.sin(angles)[:, None, :]
    first_half = values[..., :half_dim]
    second_half = values[..., half_dim:]
    return jnp.concatenate(
        [first_half * cosine - second_half * sines, second_half * cosine + first_half * sines],
        axis=-1,
    )


def project(
    tokens,
    in_gain,
    w_query,
    key_projection_weight,
    value_projection_weight,
    q_gain,
    k_gain,
    positions,
):
    tok_count = tokens.shape[0]
    tokens_wide = tokens.astype(jnp.float32)
    normed = (tokens_wide * rms_scale(tokens_wide) * in_gain).astype(jnp.bfloat16)
    queries = jnp.dot(normed, w_query, preferred_element_type=jnp.float32).reshape(
        tok_count, -1, HEAD_SIZE
    )
    queries = rotate(queries * rms_scale(queries) * q_gain, positions).astype(jnp.bfloat16)
    fresh_key_rows = jnp.dot(
        normed, key_projection_weight, preferred_element_type=jnp.float32
    ).reshape(tok_count, -1, HEAD_SIZE)
    fresh_key_rows = rotate(fresh_key_rows * rms_scale(fresh_key_rows) * k_gain, positions).astype(
        jnp.bfloat16
    )
    fresh_value_rows = jnp.dot(
        normed, value_projection_weight, preferred_element_type=jnp.float32
    ).reshape(tok_count, -1, HEAD_SIZE)
    fresh_value_rows = (fresh_value_rows * rms_scale(fresh_value_rows)).astype(jnp.bfloat16)
    return (
        normed,
        queries,
        fresh_key_rows.reshape(tok_count, HEAD_SIZE),
        fresh_value_rows.reshape(tok_count, HEAD_SIZE),
    )


def greet(devices):
    barrier = pltpu.get_barrier_semaphore()
    for device in devices:
        pl.semaphore_signal(barrier, inc=1, device_id={"page": device}, device_id_type=MESH)
    pl.semaphore_wait(barrier, len(devices))


def gather_kernel(blocks, fresh, q, fresh_all, q_all, local_sem, send, recv, q_send, q_recv):
    me = lax.axis_index("page")
    mine = lax.rem(me, PLANE)
    block = lax.div(me, PLANE)
    base = block * PLANE
    z_peers = [lax.rem(block + d, blocks) * PLANE + mine for d in range(1, blocks)]
    peers = [base + lax.rem(mine + d, PLANE) for d in range(1, PLANE)]
    greet([*z_peers, *peers])
    started = []
    for d in range(1, blocks):
        started.append(
            pltpu.make_async_remote_copy(
                src_ref=q,
                dst_ref=q_all.at[d],
                send_sem=q_send.at[d - 1],
                recv_sem=q_recv.at[d - 1],
                device_id={"page": z_peers[d - 1]},
                device_id_type=MESH,
            )
        )
        started[-1].start()
    for d in range(1, PLANE):
        made = pltpu.make_async_remote_copy(
            src_ref=fresh,
            dst_ref=fresh_all.at[mine],
            send_sem=send.at[d - 1],
            recv_sem=recv.at[d - 1],
            device_id={"page": peers[d - 1]},
            device_id_type=MESH,
        )
        made.start()
        started.append(made)
    own = [
        pltpu.make_async_copy(fresh, fresh_all.at[mine], local_sem.at[0]),
        pltpu.make_async_copy(q, q_all.at[0], local_sem.at[1]),
    ]
    for made in own:
        made.start()
    for made in started[: blocks - 1]:
        made.wait_recv()
    for d in range(1, PLANE):
        pltpu.make_async_remote_copy(
            src_ref=fresh,
            dst_ref=fresh_all.at[lax.rem(mine + PLANE - d, PLANE)],
            send_sem=send.at[d - 1],
            recv_sem=recv.at[d - 1],
            device_id={"page": peers[d - 1]},
            device_id_type=MESH,
        ).wait_recv()
    for made in started:
        made.wait_send()
    for made in own:
        made.wait()


def gather(fresh, q, blocks):
    return pl.pallas_call(
        functools.partial(gather_kernel, blocks),
        out_shape=[
            jax.ShapeDtypeStruct((PLANE, *fresh.shape), fresh.dtype),
            jax.ShapeDtypeStruct((blocks, *q.shape), q.dtype),
        ],
        in_specs=[ANY] * 2,
        out_specs=[ANY] * 2,
        scratch_shapes=[
            pltpu.SemaphoreType.DMA((2,)),
            pltpu.SemaphoreType.DMA((PLANE - 1,)),
            pltpu.SemaphoreType.DMA((PLANE - 1,)),
            pltpu.SemaphoreType.DMA((blocks - 1,)),
            pltpu.SemaphoreType.DMA((blocks - 1,)),
        ],
        compiler_params=pltpu.CompilerParams(collective_id=0, has_side_effects=True),
        cost_estimate=pl.CostEstimate(flops=40 * 10**9, bytes_accessed=10**6, transcendentals=0),
    )(fresh, q)


def attend_kernel(
    slots, first, places, info, *refs
):
    parts = refs[:PLANE]
    fresh, q_ref, out_ref, stat_ref, keys, values, top, total, mixed, sem = refs[-10:]
    step = pl.program_id(0)
    prefix_rows = slots * PAGE_TOKENS
    part_rows = fresh.shape[2]
    suffix_rows = PLANE * part_rows
    part_slots = slots // PLANE
    entry = (first + step) * 8

    @pl.when(step == 0)
    def _():
        values[prefix_rows + suffix_rows :, :] = jnp.zeros((CHUNK, HEAD_SIZE), jnp.bfloat16)
        moves = []
        for n in range(PLANE):
            for which, whole in enumerate((keys, values)):
                there = pl.ds(prefix_rows + n * part_rows, part_rows)
                moves.append((fresh.at[n, which], whole.at[there, :]))
        for n in range(slots):
            source = pl.ds((n % part_slots) * PAGE_TOKENS, PAGE_TOKENS)
            there = pl.ds(pl.multiple_of(places[n] * PAGE_TOKENS, PAGE_TOKENS), PAGE_TOKENS)
            for which, whole in enumerate((keys, values)):
                moves.append((parts[n // part_slots].at[which, source, :], whole.at[there, :]))
        moves = [pltpu.make_async_copy(*move, sem.at[n]) for n, move in enumerate(moves)]
        for move in moves:
            move.start()
        for move in moves:
            move.wait()

    top[...] = jnp.full_like(top, masked_low)
    total[...] = jnp.zeros_like(total)
    mixed[...] = jnp.zeros_like(mixed)
    rows = q_ref.shape[1]
    prefix_low, prefix_high = info[entry], info[entry + 1]
    suffix_low, suffix_high = info[entry + 2], info[entry + 3]
    first_token = info[entry + 4]

    def fold(offset, valid):
        offset = pl.multiple_of(offset, PAGE_TOKENS)
        scores = lax.dot_general(
            keys[pl.ds(offset, CHUNK), :],
            q_ref[0],
            (((1,), (1,)), ((), ())),
            preferred_element_type=jnp.float32,
        )
        scores = jnp.where(valid, scores, masked_low)
        row_top = jnp.maximum(top[...], jnp.max(scores, axis=0, keepdims=True))
        factor = jnp.exp(top[...] - row_top)
        weights = jnp.exp(scores - row_top)
        total[...] = total[...] * factor + jnp.sum(weights, axis=0, keepdims=True)
        mixed[...] = mixed[...] * factor + lax.dot_general(
            values[pl.ds(offset, CHUNK), :],
            weights.astype(jnp.bfloat16),
            (((0,), (0,)), ((), ())),
            preferred_element_type=jnp.float32,
        )
        top[...] = row_top

    in_chunk = lax.broadcasted_iota(jnp.int32, (CHUNK, rows), 0)
    token = lax.rem(lax.broadcasted_iota(jnp.int32, (CHUNK, rows), 1), PAGE_TOKENS)
    chunk_pages = CHUNK // PAGE_TOKENS

    def prefix_step(n, _):
        start = (prefix_low + n * chunk_pages) * PAGE_TOKENS
        fold(start, in_chunk < prefix_high * PAGE_TOKENS - start)
        return 0

    def suffix_step(n, _):
        start = (suffix_low + n * chunk_pages) * PAGE_TOKENS
        valid = (in_chunk < suffix_high * PAGE_TOKENS - start) & (
            in_chunk - token <= first_token - start
        )
        fold(start + prefix_rows, valid)
        return 0

    lax.fori_loop(0, lax.div(prefix_high - prefix_low + chunk_pages - 1, chunk_pages), prefix_step, 0)
    lax.fori_loop(0, lax.div(suffix_high - suffix_low + chunk_pages - 1, chunk_pages), suffix_step, 0)
    scale = jnp.where(total[...] > 0, 1.0 / jnp.maximum(total[...], 1e-30), 0.0)
    out_ref[0] = (mixed[...] * scale).astype(jnp.bfloat16)
    stat_ref[0, 0:1, :] = top[...]
    stat_ref[0, 1:2, :] = total[...]
    stat_ref[0, 2:8, :] = jnp.zeros((6, rows), jnp.float32)


def attend(places, info, parts, fresh, after, queries, first, pages):
    _, rows, _ = queries.shape
    slots = places.shape[0]
    span = (slots * PAGE_TOKENS) + PLANE * fresh.shape[2] + CHUNK
    return pl.pallas_call(
        functools.partial(attend_kernel, slots, first),
        out_shape=[
            jax.ShapeDtypeStruct((pages, HEAD_SIZE, rows), jnp.bfloat16),
            jax.ShapeDtypeStruct((pages, 8, rows), jnp.float32),
        ],
        grid_spec=pltpu.PrefetchScalarGridSpec(
            num_scalar_prefetch=2,
            grid=(pages,),
            in_specs=[ANY] * (PLANE + 1 + len(after))
            + [pl.BlockSpec((1, rows, HEAD_SIZE), lambda i, *_: (first + i, 0, 0))],
            out_specs=[
                pl.BlockSpec((1, HEAD_SIZE, rows), lambda i, *_: (i, 0, 0)),
                pl.BlockSpec((1, 8, rows), lambda i, *_: (i, 0, 0)),
            ],
            scratch_shapes=[
                pltpu.VMEM((span, HEAD_SIZE), jnp.bfloat16),
                pltpu.VMEM((span, HEAD_SIZE), jnp.bfloat16),
                pltpu.VMEM((1, rows), jnp.float32),
                pltpu.VMEM((1, rows), jnp.float32),
                pltpu.VMEM((HEAD_SIZE, rows), jnp.float32),
                pltpu.SemaphoreType.DMA((2 * slots + 2 * PLANE,)),
            ],
        ),
        compiler_params=pltpu.CompilerParams(vmem_limit_bytes=VMEM_LIMIT),
        cost_estimate=pl.CostEstimate(
            flops=10**8, bytes_accessed=10**5, transcendentals=0
        ),
    )(places, info, *parts, *after, fresh, queries)


def moved(block, axis_size, target):
    return lax.ppermute(block, "page", [(p, target(p)) for p in range(axis_size)])


def page_facts(pages, page_lengths, request_group):
    ids = jnp.arange(page_lengths.shape[0])
    starts = jnp.sum(jnp.where(ids[None, :] < ids[:, None], page_lengths[None, :], 0), axis=1)
    belongs = (pages[:, None] >= starts[None, :]) & (
        pages[:, None] < (starts + page_lengths)[None, :]
    )
    first = jnp.sum(jnp.where(belongs, starts[None, :], 0), axis=1)
    group = jnp.sum(jnp.where(belongs, request_group[None, :], 0), axis=1)
    return first, group


def local(
    tokens,
    in_gain,
    w_query,
    key_projection_weight,
    value_projection_weight,
    q_gain,
    k_gain,
    w_out,
    post_gain,
    laurel_left,
    laurel_right,
    laurel_gain,
    prefix_key_slots,
    prefix_value_slots,
    prefix_slot_map,
    page_lengths,
    request_group,
    suffix_page_map,
):
    tok_count, model_width = tokens.shape
    pages_here = tok_count // PAGE_TOKENS
    device = lax.axis_index("page")
    blocks = lax.axis_size("page") // PLANE
    mine = device % PLANE
    block = device // PLANE
    heads = w_query.shape[1] // HEAD_SIZE
    plane_pages = PLANE * pages_here

    my_pages = device * pages_here + jnp.arange(pages_here, dtype=jnp.int32)
    my_first, _ = page_facts(my_pages, page_lengths, request_group)
    position = (
        (my_pages - my_first)[:, None] * PAGE_TOKENS + jnp.arange(PAGE_TOKENS, dtype=jnp.int32)
    ).reshape(tok_count)
    normed, queries, fresh_key_rows, fresh_value_rows = project(
        tokens,
        in_gain,
        w_query,
        key_projection_weight,
        value_projection_weight,
        q_gain,
        k_gain,
        position + PREFIX_TOKENS,
    )
    local_slot = suffix_page_map - device * pages_here

    def place(rows):
        paged = rows.reshape(pages_here, PAGE_TOKENS, HEAD_SIZE)
        parts = []
        for slot in range(pages_here):
            part = paged[0]
            for n in range(1, pages_here):
                part = jnp.where(local_slot[n] == slot, paged[n], part)
            parts.append(part)
        return jnp.concatenate(parts, axis=0)

    suffix_key_cache = place(fresh_key_rows)
    suffix_value_cache = place(fresh_value_rows)

    slots = PLANE * prefix_key_slots.shape[0] // PAGE_TOKENS
    part_slots = slots // PLANE
    slot_parts = jnp.arange(slots, dtype=jnp.int32) // part_slots
    slot_ids = (block * PLANE + (mine ^ slot_parts)) * part_slots + jnp.arange(
        slots, dtype=jnp.int32
    ) % part_slots
    map_group = jnp.arange(prefix_slot_map.shape[0], dtype=jnp.int32) // PREFIX_PAGES
    slot_group = jnp.sum(
        jnp.where(slot_ids[:, None] == prefix_slot_map[None, :], map_group[None, :], 0), axis=1
    )
    order = jnp.arange(slots, dtype=jnp.int32)
    ahead = (slot_group[None, :] < slot_group[:, None]) | (
        (slot_group[None, :] == slot_group[:, None]) & (order[None, :] < order[:, None])
    )
    places = jnp.sum(ahead.astype(jnp.int32), axis=1)
    q_pages = (
        ((block + blocks - jnp.arange(blocks, dtype=jnp.int32)) % blocks * PLANE + mine)[:, None]
        * pages_here
        + jnp.arange(pages_here, dtype=jnp.int32)
    ).reshape(-1)
    q_first, q_group = page_facts(q_pages, page_lengths, request_group)
    prefix_low = jnp.sum((slot_group[None, :] < q_group[:, None]).astype(jnp.int32), axis=1)
    prefix_high = jnp.sum((slot_group[None, :] <= q_group[:, None]).astype(jnp.int32), axis=1)
    plane_first = block * plane_pages
    suffix_low = jnp.maximum(q_first - plane_first, 0)
    suffix_high = jnp.minimum(q_pages + 1 - plane_first, plane_pages)
    suffix_low = jnp.minimum(suffix_low, plane_pages)
    suffix_high = jnp.maximum(suffix_high, suffix_low)
    first_token = (q_pages - plane_first) * PAGE_TOKENS
    nothing = jnp.zeros_like(first_token)
    info = jnp.stack(
        [prefix_low, prefix_high, suffix_low, suffix_high, first_token, nothing, nothing, nothing],
        axis=1,
    ).reshape(-1)

    paged_queries = queries.reshape(pages_here, PAGE_TOKENS, heads, HEAD_SIZE).transpose(0, 2, 1, 3)
    paged_queries = paged_queries.reshape(pages_here * heads * PAGE_TOKENS, HEAD_SIZE)
    size = lax.axis_size("page")
    prefix = jnp.stack([prefix_key_slots, prefix_value_slots])
    parts = (
        prefix,
        moved(prefix, size, lambda p: p ^ 1),
        moved(prefix, size, lambda p: p ^ 2),
        moved(prefix, size, lambda p: p ^ 3),
    )
    fresh, q_all = gather(jnp.stack([fresh_key_rows, fresh_value_rows]), paged_queries, blocks)
    q_all = q_all.reshape(blocks * pages_here, heads * PAGE_TOKENS, HEAD_SIZE)
    outs, stats = [], []
    for d in [*range(1, blocks), 0]:
        out, stat = attend(
            places, info, parts, fresh, outs[-2:-1] if d else [], q_all, d * pages_here, pages_here
        )
        if d:
            back = lambda p, d=d: (p // PLANE + blocks - d) % blocks * PLANE + p % PLANE
            out, stat = moved(out, size, back), moved(stat, size, back)
        outs.append(out)
        stats.append(stat)
    out, stat = jnp.stack(outs), jnp.stack(stats)
    tops, totals = stat[:, :, 0, :], stat[:, :, 1, :]
    share = totals * jnp.exp(tops - jnp.max(tops, axis=0, keepdims=True))
    share = share / jnp.sum(share, axis=0, keepdims=True)
    attended = jnp.sum(out.astype(jnp.float32) * share[:, :, None, :], axis=0).astype(jnp.bfloat16)
    attended = (
        attended.reshape(pages_here, HEAD_SIZE, heads, PAGE_TOKENS)
        .transpose(0, 3, 2, 1)
        .reshape(tok_count, heads * HEAD_SIZE)
    )
    attn_part = jnp.dot(attended, w_out, preferred_element_type=jnp.float32).astype(jnp.bfloat16)
    other_part = lax.ppermute(attn_part, "kv", [(0, 1), (1, 0)])
    summed_out = attn_part.astype(jnp.float32) + other_part.astype(jnp.float32)
    kv_index = lax.axis_index("kv")
    half_width = model_width // lax.axis_size("kv")

    def columns(source):
        return lax.dynamic_slice_in_dim(source, kv_index * half_width, half_width, source.ndim - 1)

    low_rank = jnp.dot(normed, laurel_left, preferred_element_type=jnp.float32).astype(jnp.bfloat16)
    laurel_full = jnp.dot(low_rank, laurel_right, preferred_element_type=jnp.float32)
    laurel_part = columns(laurel_full) * rms_scale(laurel_full) * columns(laurel_gain)
    laurel = columns(normed).astype(jnp.float32) + laurel_part
    attn_branch = columns(summed_out) * rms_scale(summed_out) * columns(post_gain)
    layer_out = (
        (columns(tokens).astype(jnp.float32) + attn_branch + laurel) * 2.0 ** (-0.5)
    ).astype(jnp.bfloat16)
    return (layer_out, suffix_key_cache, suffix_value_cache)


def solution(mesh):
    placed = (
        P("page", None),
        P(),
        P(None, "kv"),
        P(None, "kv"),
        P(None, "kv"),
        P(),
        P(),
        P("kv", None),
        P(),
        P(),
        P(),
        P(),
        P("page", "kv"),
        P("page", "kv"),
        P(),
        P(),
        P(),
        P("page"),
    )
    return jax.shard_map(
        local,
        mesh=mesh,
        in_specs=placed,
        out_specs=(P("page", "kv"), P("page", "kv"), P("page", "kv")),
        check_vma=False,
    )
```
